128 devices in a mesh: wide: 16 (over z, x), narrow: 8 (over y, core).
Axes of the slice: x: 4, y: 4, z: 4, core: 2. Of those that a mesh axis runs over, the one named last changes fastest.
Arguments:
- density: bfloat16 [4, 4096, 4096], P(None, 'wide', 'narrow'), may hold values from -6 to 6
- coefficients: bfloat16 [1024, 256, 4096], P(('wide', 'narrow')), may hold values from -0.5 to 0.5
- task_blocks: int32 [1024, 2], P(('wide', 'narrow')), may hold values from 0 to 63, as said below
- task_live: int32 [128], P(('wide', 'narrow')), may hold values from 1 to 8, as said below
Outputs:
- exchange_matrix: float32 [4, 4096, 4096], P(None, 'wide', 'narrow')
The draws below stay inside these ranges and needn't reach their ends.
Inputs may be any that keep to these rules, and one draw needn't show every extreme that they name: `task_blocks`: for the device i of the joint axis wide+narrow (i = w * 8 + n), every slot's first block r lies in the block column group of n: n * 8 <= r < (n + 1) * 8. The second blocks c of the 8 slots of one device lie in 8 different stripes c // 4. A pair may occur on several devices. The live tasks of a device are its first task_live slots; some device has all 8 live.
All inputs are finite; a program needn't handle non-finite values.
Results may differ from the reference program's by a relative error of at most 0.0028.
Values may be sent and summed in bfloat16 or wider, within the bound.
A program may use at most 192 MiB of HBM per device.

```python
import jax
import jax.numpy as jnp
from jax import lax

BF = 64
AUXP = 256
NDM = 4
SBLK = 4
TASK_DEV = 8
NBLK = 64
NB = 4096
TASKS = 1024
N_WIDE = 16
N_NARROW = 8


def draw_task_blocks(key, part):
    key = jax.random.fold_in(key, 11)
    key_row, key_order, key_inner = jax.random.split(key, 3)
    device_count = N_WIDE * N_NARROW
    group = NBLK // N_NARROW
    rows = jnp.arange(TASKS, dtype=jnp.int32)
    column = rows // TASK_DEV % N_NARROW
    row_blk = column * group + jax.random.randint(key_row, (TASKS,), 0, group, dtype=jnp.int32)
    scores = jax.random.randint(key_order, (device_count, N_WIDE), 0, 1048576, dtype=jnp.int32) * N_WIDE + jnp.arange(N_WIDE, dtype=jnp.int32)[None, :]
    stripes = jnp.argsort(scores, axis=1)[:, :TASK_DEV].reshape(TASKS).astype(jnp.int32)
    col_blk = stripes * SBLK + jax.random.randint(key_inner, (TASKS,), 0, SBLK, dtype=jnp.int32)
    return jnp.stack([row_blk, col_blk], axis=1).astype(jnp.int32)


def draw_task_live(key, part):
    key = jax.random.fold_in(key, 12)
    key_load, key_busy = jax.random.split(key, 2)
    device_count = N_WIDE * N_NARROW
    spread = jax.random.randint(key_load, (device_count,), 0, TASK_DEV, dtype=jnp.int32)
    counts = 1 + spread * spread // TASK_DEV
    busiest = jax.random.randint(key_busy, (), 0, device_count, dtype=jnp.int32)
    counts = jnp.where(jnp.arange(device_count, dtype=jnp.int32) == busiest, TASK_DEV, counts)
    return counts.astype(jnp.int32)


def block_scale(rng, dims, cuts, smallest, top_value):
    def one(dim, shards_of):
        heights = jax.random.uniform(jax.random.fold_in(jax.random.fold_in(rng, 6), dim), (shards_of,), jnp.float32, smallest / len(cuts), top_value / len(cuts))
        return jnp.repeat(jnp.exp(heights), dims[dim] // shards_of).reshape((-1,) + (1,) * (len(dims) - dim - 1))

    gain = one(*cuts[0])
    for cut in cuts[1:]:
        gain = gain * one(*cut)
    return gain


def gaussian(key, dims, scale, bound, pieces=(), held_as=jnp.bfloat16):
    entries = jax.random.normal(key, dims, jnp.float32) * scale
    if len(pieces) > 0:
        entries = block_scale(key, dims, pieces, -0.22, 0.18) * entries
    return jnp.clip(entries, min=-bound, max=bound).astype(held_as)


def setup_inputs(seed: int = 0) -> dict:
    seeds = jax.random.split(jax.random.key(seed), 5)
    return {
        "density": gaussian(seeds[0], (NDM, NB, NB), 1.0, 6.0, ((1, 16), (2, 8))),
        "coefficients": gaussian(seeds[1], (TASKS, AUXP, BF * BF), 0.03125, 0.5, ((0, 128),)),
        "task_blocks": draw_task_blocks(jax.random.fold_in(seeds[4], 71), 0),
        "task_live": draw_task_live(jax.random.fold_in(seeds[4], 71), 0),
    }


def reference(density, coefficients, task_blocks, task_live):
    zero_index = jnp.zeros((), jnp.int32)
    totals = jnp.zeros((NDM, NBLK * BF, NBLK * BF), jnp.float32)
    numbers = jnp.arange(TASKS, dtype=jnp.int32)

    def one_task(running, items):
        number, coef_rows, pair = items
        alive = number % TASK_DEV < task_live[number // TASK_DEV]

        def add_term(current):
            row_blk = pair[0].astype(jnp.int32)
            col_blk = pair[1].astype(jnp.int32)
            coef_mat = coef_rows.reshape(AUXP, BF, BF).astype(jnp.float32)
            dens_blk = lax.dynamic_slice(density, (zero_index, col_blk * BF, row_blk * BF), (NDM, BF, BF)).astype(jnp.float32)
            halves = jnp.einsum("pml,dls->pmds", coef_mat, dens_blk)
            halves = lax.optimization_barrier(halves.astype(jnp.bfloat16)).astype(jnp.float32)
            term = jnp.einsum("pmds,psn->dmn", halves, coef_mat)
            corner = (zero_index, row_blk * BF, col_blk * BF)
            before = lax.dynamic_slice(current, corner, (NDM, BF, BF))
            return lax.dynamic_update_slice(current, before + term, corner)

        return lax.cond(alive, add_term, lambda current: current, running), None

    totals, unused = lax.scan(one_task, totals, (numbers, coefficients, task_blocks))
    return totals
```

```python
import jax
import jax.numpy as jnp
from jax import lax
from jax.experimental import pallas as pl
from jax.experimental.pallas import tpu as pltpu
from jax.sharding import PartitionSpec as P

BF = 64
AUXP = 256
NDM = 4
SLOTS = 8
N_WIDE = 16
N_NARROW = 8
BF16 = jnp.bfloat16
F32 = jnp.float32
MESH = pl.DeviceIdType.MESH
NT = (((1,), (1,)), ((), ()))
NN = (((1,), (0,)), ((), ()))


def iota(shape, dim):
    return lax.broadcasted_iota(jnp.int32, shape, dim)


def one_hot(hit):
    return jnp.where(hit, 1.0, 0.0).astype(BF16)


def build_info(blocks, live):
    lane = iota((8, 128), 1)
    row = iota((8, 128), 0)
    info = jnp.where(row == 0, -1, 0)
    alive = lane * 0 + live[0]
    for t in range(SLOTS):
        r, c = blocks[t, 0], blocks[t, 1]
        hit = (lane == lax.div(c, 4)) & (t < alive)
        info = jnp.where(hit & (row == 0), r * 64 + c, info)
        info = jnp.where(hit & (row == 1), t, info)
    return info


def pack_block(dens, code):
    code = jnp.maximum(code, 0)
    r, c = lax.div(code, 64), lax.rem(code, 64)
    pair = dens[lax.rem(c, 4), lax.div(lax.rem(r, 8), 2)].astype(F32)
    lane = iota((BF, 128), 1)
    odd = lane * 0 + lax.rem(r, 2) == 1
    parts = []
    for d in range(NDM):
        turned = pltpu.roll(pair[d], BF, 1)
        if d % 2 == 0:
            parts.append(jnp.where(odd, turned, pair[d]))
        else:
            parts.append(jnp.where(odd, pair[d], turned))
    low = lane < BF
    first = jnp.where(low, parts[0], parts[1])
    second = jnp.where(low, parts[2], parts[3])
    return jnp.concatenate([first, second], axis=1).astype(BF16)


def spread_block(block, perm, dz):
    tall = jnp.concatenate([block] * 4, axis=0)
    turned = lax.dot_general(perm[...], tall, NT, preferred_element_type=F32).astype(BF16)
    part = iota((256, 256), 1) // BF
    for q in range(4):
        dz[q] = jnp.where(part == q, turned, jnp.zeros_like(turned))


def task_term(coef, dz, half):
    groups = 16
    tall = jnp.concatenate([coef[:, g * 256:(g + 1) * 256] for g in range(groups)], axis=0)
    for q in range(4):
        rows = lax.dot_general(dz[q], tall, NT, preferred_element_type=F32).astype(BF16)
        for g in range(groups):
            half[g * 4 + q] = rows[:, g * 256:(g + 1) * 256]
    left = jnp.concatenate(
        [half[:, j * 16:(j + 1) * 16, :].reshape(BF * 16, AUXP) for j in range(16)], axis=1
    )
    right = jnp.concatenate([coef[:, j * 256:(j + 1) * 256] for j in range(16)], axis=0)
    full = lax.dot_general(left, right, NN, preferred_element_type=F32)
    full = full.reshape(BF, 2, 8, 256)
    both = full[:, 0, :, :128] + full[:, 1, :, 128:]
    keep = iota((8, 128), 0) // 4 == iota((8, 128), 1) // BF
    both = jnp.where(keep[None], both, 0.0)
    return both + pltpu.roll(pltpu.roll(both, BF, 2), 4, 1)


def slot_layout(folded, pick):
    flat = folded.reshape(BF * 8, 128).astype(BF16)
    even = lax.dot_general(pick[0], flat, NN, preferred_element_type=F32)
    odd = lax.dot_general(pick[1], flat, NN, preferred_element_type=F32)
    return jnp.where(iota((128, 128), 1) < BF, even, odd).astype(BF16)


def exchange_kernel(
    dens_hbm, coef_hbm, blocks, live, recv, meta,
    coef, dens, info, own, codes, codes_sm, dsend, dblk, dz, perm, pick, half, terms, slots,
    coef_sem, dens_sem, small_sem, code_send, code_recv, meta_send, meta_recv, d_send, d_recv, t_send, t_recv,
):
    w = lax.axis_index("wide")
    n = lax.axis_index("narrow")
    src_n = w // 2

    def dens_copy(k):
        i, j = k // 4, k % 4
        return pltpu.make_async_copy(
            dens_hbm.at[:, pl.ds(i * BF, BF), pl.ds(j * 128, 128)], dens.at[i, j], dens_sem.at[k]
        )

    for k in range(16):
        dens_copy(k).start()
    for t in range(SLOTS):
        pltpu.make_async_copy(coef_hbm.at[t], coef.at[t], coef_sem.at[t]).start()

    info[...] = build_info(blocks, live)
    own_copy = pltpu.make_async_copy(info, own, small_sem.at[0])
    own_copy.start()

    barrier = pltpu.get_barrier_semaphore()

    def greet_peer(k, carry):
        pl.semaphore_signal(barrier, inc=1, device_id=(lax.rem(w + k, N_WIDE), n), device_id_type=MESH)
        return carry

    lax.fori_loop(1, N_WIDE, greet_peer, 0)

    def greet_source(k, carry):
        @pl.when(jnp.logical_or(k != w, src_n != n))
        def _():
            pl.semaphore_signal(barrier, inc=1, device_id=(k, src_n), device_id_type=MESH)
        return carry

    lax.fori_loop(0, N_WIDE, greet_source, 0)

    @pl.when(src_n == n)
    def _():
        pl.semaphore_wait(barrier, 2 * N_WIDE - 2)

    @pl.when(src_n != n)
    def _():
        pl.semaphore_wait(barrier, 2 * N_WIDE - 1)

    def code_copy(k):
        peer = lax.rem(w + k, N_WIDE)
        return pltpu.make_async_remote_copy(
            src_ref=info, dst_ref=codes.at[w], send_sem=code_send.at[k], recv_sem=code_recv.at[w],
            device_id=(peer, n), device_id_type=MESH,
        )

    def send_code(k, carry):
        code_copy(k).start()
        return carry

    lax.fori_loop(1, N_WIDE, send_code, 0)
    codes[w] = info[...]

    def meta_copy(j):
        return pltpu.make_async_remote_copy(
            src_ref=info, dst_ref=meta.at[w], send_sem=meta_send.at[j], recv_sem=meta_recv.at[w],
            device_id=(2 * n + j // N_NARROW, j % N_NARROW), device_id_type=MESH,
        )

    def is_self(j):
        return jnp.logical_and(2 * n + j // N_NARROW == w, j % N_NARROW == n)

    def send_meta(j, carry):
        @pl.when(is_self(j))
        def _():
            pltpu.make_async_copy(info, meta.at[w], meta_recv.at[w]).start()

        @pl.when(jnp.logical_not(is_self(j)))
        def _():
            meta_copy(j).start()
        return carry

    i, k = iota((256, 256), 0), iota((256, 256), 1)
    perm[...] = one_hot(k == (i % 4) * BF + i // 4)
    i, k = iota((128, 512), 0), iota((128, 512), 1)
    pick[0] = one_hot(k == (i % BF) * 8 + i // BF)
    pick[1] = one_hot(k == (i % BF) * 8 + 6 + i // BF)

    def wait_code(k, carry):
        peer = lax.rem(w + k, N_WIDE)
        pltpu.make_async_copy(info, codes.at[peer], code_recv.at[peer]).wait()
        return carry

    lax.fori_loop(1, N_WIDE, wait_code, 0)
    codes_copy = pltpu.make_async_copy(codes, codes_sm, small_sem.at[1])
    codes_copy.start()
    lax.fori_loop(0, N_WIDE, send_meta, 0)
    for k in range(16):
        dens_copy(k).wait()
    own_copy.wait()
    codes_copy.wait()

    def block_copy(k):
        peer = lax.rem(w + k, N_WIDE)
        return pltpu.make_async_remote_copy(
            src_ref=dsend.at[k], dst_ref=dblk.at[w], send_sem=d_send.at[k], recv_sem=d_recv.at[w],
            device_id=(peer, n), device_id_type=MESH,
        )

    def send_block(k, carry):
        peer = lax.rem(w + k, N_WIDE)
        dsend[k] = pack_block(dens, codes_sm[peer, 0, w])
        block_copy(k).start()
        return carry

    lax.fori_loop(1, N_WIDE, send_block, 0)
    dblk[w] = pack_block(dens, codes_sm[w, 0, w])

    def wait_block(k, carry):
        peer = lax.rem(w + k, N_WIDE)
        pltpu.make_async_copy(dsend.at[k], dblk.at[peer], d_recv.at[peer]).wait()
        return carry

    lax.fori_loop(1, N_WIDE, wait_block, 0)

    def run_task(t, carry):
        pltpu.make_async_copy(coef_hbm.at[t], coef.at[t], coef_sem.at[t]).wait()
        spread_block(dblk[lax.div(blocks[t, 1], 4)], perm, dz)
        terms[t] = slot_layout(task_term(coef.at[t], dz, half), pick)
        return carry

    lax.fori_loop(0, SLOTS, run_task, 0)

    def term_copy(j):
        return pltpu.make_async_remote_copy(
            src_ref=slots.at[j % N_NARROW], dst_ref=recv.at[w], send_sem=t_send.at[j], recv_sem=t_recv.at[w],
            device_id=(2 * n + j // N_NARROW, j % N_NARROW), device_id_type=MESH,
        )

    def send_term(k, carry):
        q = lax.rem(n + k, N_NARROW)
        slots[q, 0] = terms[own[1, 2 * q]]
        slots[q, 1] = terms[own[1, 2 * q + 1]]
        for a in range(2):
            j = a * N_NARROW + q

            @pl.when(is_self(j))
            def _():
                pltpu.make_async_copy(slots.at[q], recv.at[w], t_recv.at[w]).start()

            @pl.when(jnp.logical_not(is_self(j)))
            def _():
                term_copy(j).start()
        return carry

    lax.fori_loop(0, N_NARROW, send_term, 0)

    def wait_in(k, carry):
        pltpu.make_async_copy(info, meta.at[k], meta_recv.at[k]).wait()
        pltpu.make_async_copy(slots.at[0], recv.at[k], t_recv.at[k]).wait()
        return carry

    lax.fori_loop(0, N_WIDE, wait_in, 0)

    def wait_out(j, carry):
        @pl.when(j > 0)
        def _():
            code_copy(j).wait_send()
            block_copy(j).wait_send()

        @pl.when(jnp.logical_not(is_self(j)))
        def _():
            meta_copy(j).wait_send()
            term_copy(j).wait_send()
        return carry

    lax.fori_loop(0, N_WIDE, wait_out, 0)


def scatter_kernel(meta, recv, out):
    wide = lax.axis_index("wide")
    narrow = lax.axis_index("narrow")
    out[...] = jnp.zeros_like(out)
    lane_half = iota((128, 128), 1) // BF

    def add_slot(k, carry):
        source, b = k // 2, k % 2
        code = meta[source, 0, 2 * narrow + b]
        r, c = code // 64, code % 64

        @pl.when(jnp.logical_and(code >= 0, r // 4 == wide))
        def _():
            here = recv[source, b].astype(F32)
            turned = pltpu.roll(here, BF, 1)
            odd = c % 2
            keep = lane_half == odd
            rows = pl.multiple_of((r % 4) * BF, BF)
            cols = pl.multiple_of(((c % 8) // 2) * 128, 128)
            for high in range(2):
                part = jnp.where(keep, jnp.where(odd == high, here, turned), 0.0)
                for low in range(2):
                    at = (2 * high + low, pl.ds(rows, BF), pl.ds(cols, 128))
                    out[at] = out[at] + part[low * BF:(low + 1) * BF]
        return carry

    lax.fori_loop(0, 2 * N_WIDE, add_slot, 0)


def local(density, coefficients, task_blocks, task_live):
    any_space = pl.BlockSpec(memory_space=pl.ANY)
    smem = pl.BlockSpec(memory_space=pltpu.SMEM)
    vmem = pl.BlockSpec(memory_space=pltpu.VMEM)
    dma = pltpu.SemaphoreType.DMA
    recv, meta = pl.pallas_call(
        exchange_kernel,
        out_shape=[
            jax.ShapeDtypeStruct((N_WIDE, 2, 128, 128), BF16),
            jax.ShapeDtypeStruct((N_WIDE, 8, 128), jnp.int32),
        ],
        in_specs=[any_space, any_space, smem, smem],
        out_specs=[any_space, any_space],
        scratch_shapes=[
            pltpu.VMEM((SLOTS, AUXP, BF * BF), BF16),
            pltpu.VMEM((4, 4, NDM, BF, 128), BF16),
            pltpu.VMEM((8, 128), jnp.int32),
            pltpu.SMEM((8, 128), jnp.int32),
            pltpu.VMEM((N_WIDE, 8, 128), jnp.int32),
            pltpu.SMEM((N_WIDE, 8, 128), jnp.int32),
            pltpu.VMEM((N_WIDE, BF, 256), BF16),
            pltpu.VMEM((N_WIDE, BF, 256), BF16),
            pltpu.VMEM((4, 256, 256), BF16),
            pltpu.VMEM((256, 256), BF16),
            pltpu.VMEM((2, 128, 512), BF16),
            pltpu.VMEM((BF, 256, AUXP), BF16),
            pltpu.VMEM((SLOTS, 128, 128), BF16),
            pltpu.VMEM((N_NARROW, 2, 128, 128), BF16),
            dma((SLOTS,)), dma((16,)), dma((2,)),
            dma((N_WIDE,)), dma((N_WIDE,)), dma((N_WIDE,)), dma((N_WIDE,)),
            dma((N_WIDE,)), dma((N_WIDE,)), dma((N_WIDE,)), dma((N_WIDE,)),
        ],
        compiler_params=pltpu.CompilerParams(
            collective_id=0, has_side_effects=True, vmem_limit_bytes=56 * 2**20
        ),
        name="exchange",
    )(density, coefficients, task_blocks, task_live)
    return pl.pallas_call(
        scatter_kernel,
        out_shape=jax.ShapeDtypeStruct(density.shape, F32),
        in_specs=[smem, vmem],
        out_specs=vmem,
        compiler_params=pltpu.CompilerParams(vmem_limit_bytes=32 * 2**20),
        name="scatter",
    )(meta, recv)


def solution(mesh):
    in_specs = (
        P(None, "wide", "narrow"),
        P(("wide", "narrow"), None, None),
        P(("wide", "narrow"), None),
        P(("wide", "narrow")),
    )
    out_specs = P(None, "wide", "narrow")
    return jax.shard_map(local, mesh=mesh, in_specs=in_specs, out_specs=out_specs, check_vma=False)
```

```python
import jax
import jax.numpy as jnp
from jax import lax
from jax.experimental import pallas as pl
from jax.experimental.pallas import tpu as pltpu
from jax.sharding import PartitionSpec as P

BF = 64
AUXP = 256
NDM = 4
SLOTS = 8
N_WIDE = 16
N_NARROW = 8
BF16 = jnp.bfloat16
F32 = jnp.float32
MESH = pl.DeviceIdType.MESH
PASSES = ((0, 10), (10, 6))
NT = (((1,), (1,)), ((), ()))
NN = (((1,), (0,)), ((), ()))


def iota(shape, dim):
    return lax.broadcasted_iota(jnp.int32, shape, dim)


def one_hot(hit):
    return jnp.where(hit, 1.0, 0.0).astype(BF16)


def build_info(blocks, live):
    lane = iota((8, 128), 1)
    row = iota((8, 128), 0)
    info = jnp.where(row == 0, -1, 0)
    alive = lane * 0 + live[0]
    for t in range(SLOTS):
        r, c = blocks[0, t], blocks[1, t]
        hit = (lane == lax.div(c, 4)) & (t < alive)
        info = jnp.where(hit & (row == 0), r * 64 + c, info)
        info = jnp.where(hit & (row == 1), t, info)
    return info


def pack_block(dens, code):
    code = jnp.maximum(code, 0)
    r, c = lax.div(code, 64), lax.rem(code, 64)
    pair = dens[lax.rem(c, 4), lax.div(lax.rem(r, 8), 2)].astype(F32)
    lane = iota((BF, 128), 1)
    odd = lane * 0 + lax.rem(r, 2) == 1
    parts = []
    for d in range(NDM):
        turned = pltpu.roll(pair[d], BF, 1)
        if d % 2 == 0:
            parts.append(jnp.where(odd, turned, pair[d]))
        else:
            parts.append(jnp.where(odd, pair[d], turned))
    low = lane < BF
    first = jnp.where(low, parts[0], parts[1])
    second = jnp.where(low, parts[2], parts[3])
    return jnp.concatenate([first, second], axis=1).astype(BF16)


def spread_block(block, perm, dz):
    tall = jnp.concatenate([block] * 4, axis=0)
    turned = lax.dot_general(perm[...], tall, NT, preferred_element_type=F32).astype(BF16)
    part = iota((256, 256), 1) // BF
    for q in range(4):
        dz[q] = jnp.where(part == q, turned, jnp.zeros_like(turned))


def first_step(coef, dz, half, start, groups):
    tall = jnp.concatenate(
        [coef[:, g * 256:(g + 1) * 256] for g in range(start, start + groups)], axis=0
    )
    for q in range(4):
        rows = lax.dot_general(dz[q], tall, NT, preferred_element_type=F32).astype(BF16)
        for g in range(groups):
            half[g * 4 + q] = rows[:, g * 256:(g + 1) * 256]


def second_step(coef, half, groups):
    m = 4 * groups
    left = jnp.concatenate(
        [half[0:m, j * 16:(j + 1) * 16, :].reshape(m * 16, AUXP) for j in range(16)], axis=1
    )
    right = jnp.concatenate([coef[:, j * 256:(j + 1) * 256] for j in range(16)], axis=0)
    full = lax.dot_general(left, right, NN, preferred_element_type=F32)
    full = full.reshape(m, 2, 8, 256)
    both = full[:, 0, :, :128] + full[:, 1, :, 128:]
    keep = iota((8, 128), 0) // 4 == iota((8, 128), 1) // BF
    both = jnp.where(keep[None], both, 0.0)
    folded = both + pltpu.roll(pltpu.roll(both, BF, 2), 4, 1)
    flat = folded.reshape(m * 8, 128).astype(BF16)
    i, k = iota((2 * m, m * 8), 0), iota((2 * m, m * 8), 1)
    even = one_hot(k == (i % m) * 8 + i // m)
    odd = one_hot(k == (i % m) * 8 + 6 + i // m)
    even = lax.dot_general(even, flat, NN, preferred_element_type=F32)
    odd = lax.dot_general(odd, flat, NN, preferred_element_type=F32)
    return jnp.where(iota((2 * m, 128), 1) < BF, even, odd).astype(BF16)


def label(code):
    lane = iota((16, 128), 1)
    code = lane * 0 + code
    r, c = lax.div(code, jnp.full_like(code, 64)), lax.rem(code, jnp.full_like(code, 64))
    value = jnp.where(lane == 0, r, jnp.where(lane == 1, c, jnp.where(code >= 0, 1, 0)))
    return value.astype(F32).astype(BF16)


def exchange_kernel(
    dens_hbm, coef_hbm, blocks, live, *refs
):
    count = len(PASSES)
    recvs, refs = refs[:count], refs[count:]
    terms, slots, refs = refs[:count], refs[count:2 * count], refs[2 * count:]
    (
        coef, dens, info, own, codes, codes_sm, dsend, dblk, dz, perm, half, coef_sem, dens_sem, small_sem,
        code_send, code_recv, d_send, d_recv, t_send, t_recv,
    ) = refs
    w = lax.axis_index("wide")
    n = lax.axis_index("narrow")
    src_n = lax.div(w, 2)

    def dens_copy(k):
        i, j = k // 4, k % 4
        return pltpu.make_async_copy(
            dens_hbm.at[:, pl.ds(i * BF, BF), pl.ds(j * 128, 128)], dens.at[i, j], dens_sem.at[k]
        )

    for k in range(16):
        dens_copy(k).start()
    info[...] = build_info(blocks, live)
    own_copy = pltpu.make_async_copy(info, own, small_sem.at[0])
    own_copy.start()

    barrier = pltpu.get_barrier_semaphore()

    for k in range(1, N_WIDE):
        pl.semaphore_signal(barrier, inc=1, device_id=(lax.rem(w + k, N_WIDE), n), device_id_type=MESH)
    for k in range(N_WIDE):

        @pl.when(jnp.logical_or(k != w, src_n != n))
        def _():
            pl.semaphore_signal(barrier, inc=1, device_id=(k, src_n), device_id_type=MESH)

    @pl.when(src_n == n)
    def _():
        pl.semaphore_wait(barrier, 2 * N_WIDE - 2)

    @pl.when(src_n != n)
    def _():
        pl.semaphore_wait(barrier, 2 * N_WIDE - 1)

    def code_copy(k):
        peer = lax.rem(w + k, N_WIDE)
        return pltpu.make_async_remote_copy(
            src_ref=info, dst_ref=codes.at[w], send_sem=code_send.at[k], recv_sem=code_recv.at[w],
            device_id=(peer, n), device_id_type=MESH,
        )

    for k in range(1, N_WIDE):
        code_copy(k).start()
    codes[w] = info[...]

    i, k = iota((256, 256), 0), iota((256, 256), 1)
    perm[...] = one_hot(k == (i % 4) * BF + i // 4)

    for k in range(1, N_WIDE):
        peer = lax.rem(w + k, N_WIDE)
        pltpu.make_async_copy(info, codes.at[peer], code_recv.at[peer]).wait()
    codes_copy = pltpu.make_async_copy(codes.at[:, pl.ds(0, 1), :], codes_sm, small_sem.at[1])
    codes_copy.start()
    for k in range(16):
        dens_copy(k).wait()
    own_copy.wait()
    codes_copy.wait()

    def block_copy(k):
        peer = lax.rem(w + k, N_WIDE)
        return pltpu.make_async_remote_copy(
            src_ref=dsend.at[k], dst_ref=dblk.at[w], send_sem=d_send.at[k], recv_sem=d_recv.at[w],
            device_id=(peer, n), device_id_type=MESH,
        )

    for k in range(1, N_WIDE):
        dsend[k] = pack_block(dens, codes_sm[lax.rem(w + k, N_WIDE), 0, w])
        block_copy(k).start()
    dblk[w] = pack_block(dens, codes_sm[w, 0, w])
    for t in range(SLOTS):
        pltpu.make_async_copy(coef_hbm.at[t], coef.at[t], coef_sem.at[t]).start()
    for k in range(1, N_WIDE):
        peer = lax.rem(w + k, N_WIDE)
        pltpu.make_async_copy(dsend.at[k], dblk.at[peer], d_recv.at[peer]).wait()

    def wait_coef(t):
        pltpu.make_async_copy(coef_hbm.at[t], coef.at[t], coef_sem.at[t]).wait()

    def term_copy(i, a, q):
        return pltpu.make_async_remote_copy(
            src_ref=slots[i].at[q], dst_ref=recvs[i].at[w],
            send_sem=t_send.at[i, a, q], recv_sem=t_recv.at[i, w],
            device_id=(2 * n + a, q), device_id_type=MESH,
        )

    def run_pass(i):
        start, groups = PASSES[i]
        m = 4 * groups

        def task(t, carry):
            if i == 0:
                wait_coef(t)
                spread_block(dblk[lax.div(blocks[1, t], 4)], perm, dz.at[t])
            first_step(coef.at[t], dz.at[t], half, start, groups)
            terms[i][t] = second_step(coef.at[t], half, groups)
            return carry

        lax.fori_loop(0, SLOTS, task, 0)
        for k in range(N_NARROW):
            q = lax.rem(n + k, N_NARROW)
            for b in range(2):
                slots[i][q, b, 0:2 * m] = terms[i][own[1, 2 * q + b]]
                if i == 0:
                    slots[i][q, b, 2 * m:2 * m + 16] = label(own[0, 2 * q + b])
            for a in range(2):
                if k > 0:
                    term_copy(i, a, q).start()
                    continue

                @pl.when(2 * n + a == w)
                def _():
                    pltpu.make_async_copy(slots[i].at[q], recvs[i].at[w], t_recv.at[i, w]).start()

                @pl.when(2 * n + a != w)
                def _():
                    term_copy(i, a, q).start()

    for i in range(count):
        run_pass(i)

    def wait_sent(i):
        for a in range(2):
            for k in range(N_NARROW):
                q = lax.rem(n + k, N_NARROW)
                if k > 0:
                    term_copy(i, a, q).wait_send()
                    continue

                @pl.when(2 * n + a != w)
                def _():
                    term_copy(i, a, q).wait_send()

    for k in range(1, N_WIDE):
        code_copy(k).wait_send()
        block_copy(k).wait_send()
    for i in range(count):
        for k in range(N_WIDE):
            pltpu.make_async_copy(slots[i].at[0], recvs[i].at[k], t_recv.at[i, k]).wait()
        wait_sent(i)


def scatter_kernel(*refs):
    count = len(PASSES)
    recv_hbm, out, recv, (found, table, sem) = refs[:count], refs[count], refs[count + 1:2 * count + 1], refs[2 * count + 1:]
    wide = lax.axis_index("wide")
    copies = [pltpu.make_async_copy(recv_hbm[i], recv[i], sem.at[i]) for i in range(count)]
    for copy in copies:
        copy.start()
    copies[0].wait()
    m = 4 * PASSES[0][1]
    found[...] = recv[0][:, :, 2 * m:2 * m + 16, :].astype(F32).astype(jnp.int32)
    table_copy = pltpu.make_async_copy(found.at[:, :, pl.ds(0, 1), :], table, sem.at[count])
    table_copy.start()
    out[...] = jnp.zeros_like(out)
    for copy in copies[1:]:
        copy.wait()
    table_copy.wait()

    def add_slot(k, carry):
        source, b = lax.div(k, 2), lax.rem(k, 2)
        r, c, there = (table[source, b, 0, lane] for lane in range(3))

        @pl.when(jnp.logical_and(there > 0, lax.div(r, 4) == wide))
        def _():
            odd = lax.rem(c, 2)
            rows = lax.rem(r, 4) * BF
            cols = lax.div(lax.rem(c, 8), 2) * 128
            for i in range(count):
                start, m = 4 * PASSES[i][0], 4 * PASSES[i][1]
                keep = iota((2 * m, 128), 1) // BF == odd
                here = recv[i][source, b, 0:2 * m].astype(F32)
                turned = pltpu.roll(here, BF, 1)
                for high in range(2):
                    part = jnp.where(keep, jnp.where(odd == high, here, turned), 0.0)
                    for low in range(2):
                        at = (2 * high + low, pl.ds(rows + start, m), pl.ds(cols, 128))
                        out[at] = out[at] + part[low * m:(low + 1) * m]
        return carry

    lax.fori_loop(0, 2 * N_WIDE, add_slot, 0)


def local(density, coefficients, task_blocks, task_live):
    any_space = pl.BlockSpec(memory_space=pl.ANY)
    smem = pl.BlockSpec(memory_space=pltpu.SMEM)
    dma = pltpu.SemaphoreType.DMA
    count = len(PASSES)
    sizes = [8 * groups for _, groups in PASSES]
    sent = [size + 16 * (i == 0) for i, size in enumerate(sizes)]
    recv = pl.pallas_call(
        exchange_kernel,
        out_shape=[jax.ShapeDtypeStruct((N_WIDE, 2, size, 128), BF16) for size in sent],
        in_specs=[any_space, any_space, smem, smem],
        out_specs=[any_space] * count,
        scratch_shapes=[pltpu.VMEM((SLOTS, size, 128), BF16) for size in sizes]
        + [pltpu.VMEM((N_NARROW, 2, size, 128), BF16) for size in sent]
        + [
            pltpu.VMEM((SLOTS, AUXP, BF * BF), BF16),
            pltpu.VMEM((4, 4, NDM, BF, 128), BF16),
            pltpu.VMEM((8, 128), jnp.int32),
            pltpu.SMEM((8, 128), jnp.int32),
            pltpu.VMEM((N_WIDE, 8, 128), jnp.int32),
            pltpu.SMEM((N_WIDE, 1, 128), jnp.int32),
            pltpu.VMEM((N_WIDE, BF, 256), BF16),
            pltpu.VMEM((N_WIDE, BF, 256), BF16),
            pltpu.VMEM((SLOTS, 4, 256, 256), BF16),
            pltpu.VMEM((256, 256), BF16),
            pltpu.VMEM((max(sizes) // 2, 256, AUXP), BF16),
            dma((SLOTS,)), dma((16,)), dma((2,)),
            dma((N_WIDE,)), dma((N_WIDE,)), dma((N_WIDE,)), dma((N_WIDE,)),
            dma((count, 2, N_NARROW)), dma((count, N_WIDE)),
        ],
        compiler_params=pltpu.CompilerParams(
            collective_id=0, has_side_effects=True, vmem_limit_bytes=56 * 2**20
        ),
        name="exchange",
    )(density, coefficients, task_blocks.T, task_live)
    return pl.pallas_call(
        scatter_kernel,
        out_shape=jax.ShapeDtypeStruct(density.shape, F32),
        in_specs=[any_space] * count,
        out_specs=pl.BlockSpec(memory_space=pltpu.VMEM),
        scratch_shapes=[pltpu.VMEM((N_WIDE, 2, size, 128), BF16) for size in sent]
        + [
            pltpu.VMEM((N_WIDE, 2, 16, 128), jnp.int32),
            pltpu.SMEM((N_WIDE, 2, 1, 128), jnp.int32),
            dma((count + 1,)),
        ],
        compiler_params=pltpu.CompilerParams(vmem_limit_bytes=60 * 2**20),
        name="scatter",
    )(*recv)


def solution(mesh):
    in_specs = (
        P(None, "wide", "narrow"),
        P(("wide", "narrow"), None, None),
        P(("wide", "narrow"), None),
        P(("wide", "narrow")),
    )
    out_specs = P(None, "wide", "narrow")
    return jax.shard_map(local, mesh=mesh, in_specs=in_specs, out_specs=out_specs, check_vma=False)
```

```python
import jax
import jax.numpy as jnp
from jax import lax
from jax.experimental import pallas as pl
from jax.experimental.pallas import tpu as pltpu
from jax.sharding import PartitionSpec as P

BF = 64
AUXP = 256
NDM = 4
SLOTS = 8
N_WIDE = 16
N_NARROW = 8
BF16 = jnp.bfloat16
F32 = jnp.float32
MESH = pl.DeviceIdType.MESH
PASSES = ((0, 10), (10, 6))
NT = (((1,), (1,)), ((), ()))
NN = (((1,), (0,)), ((), ()))


def iota(shape, dim):
    return lax.broadcasted_iota(jnp.int32, shape, dim)


def one_hot(hit):
    return jnp.where(hit, 1.0, 0.0).astype(BF16)


def build_info(blocks, live):
    lane = iota((8, 128), 1)
    info = jnp.full((8, 128), -1, jnp.int32)
    alive = lane * 0 + live[0]
    for t in range(SLOTS):
        r, c = blocks[0, t], blocks[1, t]
        info = jnp.where((lane == lax.div(c, 4)) & (t < alive), r * 64 + c, info)
    return info


def build_plan(blocks, info, first):
    lane = iota((8, 128), 1)
    row = iota((8, 128), 0)
    stripes = [lax.div(blocks[1, t], 4) for t in range(SLOTS)]
    keys = [lax.rem(stripe + N_WIDE - first, N_WIDE) for stripe in stripes]
    plan = jnp.where(row == 0, info, 0)
    for t in range(SLOTS):
        place = sum((keys[u] < keys[t]).astype(jnp.int32) for u in range(SLOTS) if u != t)
        plan = jnp.where((row == 1) & (lane == stripes[t]), place, plan)
        plan = jnp.where((row == 2) & (lane == place), t, plan)
        plan = jnp.where((row == 3) & (lane == place), stripes[t], plan)
    return plan


def pack_block(dens, code):
    code = jnp.maximum(code, 0)
    r, c = lax.div(code, 64), lax.rem(code, 64)
    pair = dens[lax.rem(c, 4), lax.div(lax.rem(r, 8), 2)].astype(F32)
    lane = iota((BF, 128), 1)
    odd = lane * 0 + lax.rem(r, 2) == 1
    low = lane < BF
    halves = []
    for d in range(0, NDM, 2):
        stays = jnp.where(odd, pair[d + 1], pair[d])
        moves = pltpu.roll(jnp.where(odd, pair[d], pair[d + 1]), BF, 1)
        halves.append(jnp.where(odd == low, moves, stays))
    return jnp.concatenate(halves, axis=1).astype(BF16)


def spread_block(block, perm, dz):
    tall = jnp.concatenate([block] * 4, axis=0)
    turned = lax.dot_general(perm[...], tall, NT, preferred_element_type=F32).astype(BF16)
    part = iota((256, 256), 1) // BF
    for q in range(4):
        dz[q] = jnp.where(part == q, turned, jnp.zeros_like(turned))


def first_step(coef, t, dz, half, start, groups):
    tall = jnp.concatenate(
        [coef[t, :, g * 256:(g + 1) * 256] for g in range(start, start + groups)], axis=0
    )
    for q in range(4):
        rows = lax.dot_general(dz[q], tall, NT, preferred_element_type=F32).astype(BF16)
        for g in range(groups):
            half[g * 4 + q] = rows[:, g * 256:(g + 1) * 256]


def second_step(coef, t, half, groups):
    m = 4 * groups
    left = jnp.concatenate(
        [half[0:m, j * 16:(j + 1) * 16, :].reshape(m * 16, AUXP) for j in range(16)], axis=1
    )
    right = jnp.concatenate([coef[t, :, j * 256:(j + 1) * 256] for j in range(16)], axis=0)
    full = lax.dot_general(left, right, NN, preferred_element_type=F32)
    full = full.reshape(m, 2, 8, 256)
    both = full[:, 0, :, :128] + full[:, 1, :, 128:]
    keep = iota((8, 128), 0) // 4 == iota((8, 128), 1) // BF
    both = jnp.where(keep[None], both, 0.0)
    folded = both + pltpu.roll(pltpu.roll(both, BF, 2), 4, 1)
    flat = folded.reshape(m * 8, 128).astype(BF16)
    i, k = iota((2 * m, m * 8), 0), iota((2 * m, m * 8), 1)
    even = one_hot(k == (i % m) * 8 + i // m)
    odd = one_hot(k == (i % m) * 8 + 6 + i // m)
    even = lax.dot_general(even, flat, NN, preferred_element_type=F32)
    odd = lax.dot_general(odd, flat, NN, preferred_element_type=F32)
    return jnp.where(iota((2 * m, 128), 1) < BF, even, odd).astype(BF16)


def label(code):
    lane = iota((16, 128), 1)
    code = lane * 0 + code
    r, c = lax.div(code, jnp.full_like(code, 64)), lax.rem(code, jnp.full_like(code, 64))
    value = jnp.where(lane == 0, r, jnp.where(lane == 1, c, jnp.where(code >= 0, 1, 0)))
    return value.astype(F32).astype(BF16)


def exchange_kernel(
    dens_hbm, coef_hbm, blocks, live, *refs
):
    count = len(PASSES)
    recvs, (table, *refs) = refs[:count], refs[count:]
    terms, slots, refs = refs[:count], refs[count:2 * count], refs[2 * count:]
    (
        coef, dens, info, plan, own, codes, codes_sm, dsend, dblk, dz, perm, half, labels, found, coef_sem, dens_sem, small_sem,
        code_send, code_recv, d_send, d_recv, t_send, t_recv,
    ) = refs
    w = lax.axis_index("wide")
    n = lax.axis_index("narrow")
    src_n = lax.div(w, 2)
    base = lax.rem(w + n, N_NARROW)

    def dens_copy(k):
        i, j = k // 4, k % 4
        return pltpu.make_async_copy(
            dens_hbm.at[:, pl.ds(i * BF, BF), pl.ds(j * 128, 128)], dens.at[i, j], dens_sem.at[k]
        )

    for k in range(16):
        dens_copy(k).start()
    info[...] = build_info(blocks, live)

    barrier = pltpu.get_barrier_semaphore()

    for k in range(1, N_WIDE):
        pl.semaphore_signal(barrier, inc=1, device_id=(lax.rem(w + k, N_WIDE), n), device_id_type=MESH)
    for k in range(N_WIDE):

        @pl.when(jnp.logical_or(k != w, src_n != n))
        def _():
            pl.semaphore_signal(barrier, inc=1, device_id=(k, src_n), device_id_type=MESH)

    def coef_copy(t):
        return pltpu.make_async_copy(coef_hbm.at[t], coef.at[t], coef_sem.at[t])

    for t in range(SLOTS):
        coef_copy(t).start()

    @pl.when(src_n == n)
    def _():
        pl.semaphore_wait(barrier, 2 * N_WIDE - 2)

    @pl.when(src_n != n)
    def _():
        pl.semaphore_wait(barrier, 2 * N_WIDE - 1)

    def code_copy(k):
        peer = lax.rem(w + k, N_WIDE)
        return pltpu.make_async_remote_copy(
            src_ref=info, dst_ref=codes.at[w], send_sem=code_send, recv_sem=code_recv,
            device_id=(peer, n), device_id_type=MESH,
        )

    for k in range(1, N_WIDE):
        code_copy(k).start()
    codes[w] = info[...]

    plan[...] = build_plan(blocks, info[...], 2 * base)
    own_copy = pltpu.make_async_copy(plan, own, small_sem.at[0])
    own_copy.start()

    i, k = iota((256, 256), 0), iota((256, 256), 1)
    perm[...] = one_hot(k == (i % 4) * BF + i // 4)

    most = pl.ds(0, N_WIDE - 1)
    pltpu.make_async_copy(codes.at[most], codes.at[most], code_recv).wait()
    codes_copy = pltpu.make_async_copy(codes.at[:, pl.ds(0, 1), :], codes_sm, small_sem.at[1])
    codes_copy.start()
    for k in range(16):
        dens_copy(k).wait()
    own_copy.wait()
    codes_copy.wait()

    def block_copy(k):
        peer = lax.rem(w + k, N_WIDE)
        return pltpu.make_async_remote_copy(
            src_ref=dsend.at[k], dst_ref=dblk.at[w], send_sem=d_send, recv_sem=d_recv,
            device_id=(peer, n), device_id_type=MESH,
        )

    for k in range(1, N_WIDE, 5):
        for j in range(k, k + 5):
            dsend[j] = pack_block(dens, codes_sm[lax.rem(w + j, N_WIDE), 0, w])
        for j in range(k, k + 5):
            block_copy(j).start()
    dblk[w] = pack_block(dens, codes_sm[w, 0, w])
    for t in range(SLOTS):
        coef_copy(t).wait()
    pltpu.make_async_copy(dblk.at[most], dblk.at[most], d_recv).wait()

    def term_copy(i, a, q):
        return pltpu.make_async_remote_copy(
            src_ref=slots[i].at[q], dst_ref=recvs[i].at[w],
            send_sem=t_send.at[i, a], recv_sem=t_recv.at[i],
            device_id=(2 * n + a, q), device_id_type=MESH,
        )

    def is_self(a, q):
        return jnp.logical_and(q == n, 2 * n + a == w)

    def send_terms(i, k):
        m = 4 * PASSES[i][1]
        q = lax.rem(base + k, N_NARROW)
        for b in range(2):
            slots[i][q, b, 0:2 * m] = terms[i][own[1, 2 * q + b]]
            if i == 0:
                slots[i][q, b, 2 * m:2 * m + 16] = label(own[0, 2 * q + b])
        for a in range(2):

            @pl.when(is_self(a, q))
            def _():
                pltpu.make_async_copy(slots[i].at[q], recvs[i].at[w], t_recv.at[i]).start()

            @pl.when(jnp.logical_not(is_self(a, q)))
            def _():
                term_copy(i, a, q).start()

    def run_pass(i):
        start, groups = PASSES[i]

        def task(k, carry):
            t = own[2, k]
            if i == 0:
                spread_block(dblk[own[3, k]], perm, dz.at[k])
            first_step(coef, t, dz.at[k], half, start, groups)

            def finish():
                terms[i][k] = second_step(coef, t, half, groups)

            if groups > 4:
                finish()
            else:
                pl.when(k >= 0)(finish)

            @pl.when(lax.rem(k, 2) == 1)
            def _():
                send_terms(i, lax.div(k, 2))
            return carry

        lax.fori_loop(0, SLOTS, task, 0)

        def rest(k, carry):
            send_terms(i, k)
            return carry

        lax.fori_loop(SLOTS // 2, N_NARROW, rest, 0)

    for i in range(count):
        run_pass(i)

    def wait_sent(i):
        for a in range(2):

            @pl.when(2 * n + a == w)
            def _():
                some = slots[i].at[pl.ds(0, N_NARROW - 1)]
                pltpu.make_async_copy(some, some, t_send.at[i, a]).wait()

            @pl.when(2 * n + a != w)
            def _():
                pltpu.make_async_copy(slots[i], slots[i], t_send.at[i, a]).wait()

    pltpu.make_async_copy(codes.at[most], codes.at[most], code_send).wait()
    pltpu.make_async_copy(dblk.at[most], dblk.at[most], d_send).wait()
    for i in range(count):
        pltpu.make_async_copy(recvs[i], recvs[i], t_recv.at[i]).wait()
        if i == 0:
            m = 4 * PASSES[0][1]
            label_copy = pltpu.make_async_copy(recvs[0].at[:, :, pl.ds(2 * m, 16), :], labels, small_sem.at[0])
            label_copy.start()
            label_copy.wait()
            found[...] = labels[:, :, 0:8, :].astype(F32).astype(jnp.int32)
            table_copy = pltpu.make_async_copy(found.at[:, :, pl.ds(0, 1), :], table, small_sem.at[1])
            table_copy.start()
            table_copy.wait()
        wait_sent(i)


def scatter_kernel(table_hbm, *refs):
    count = len(PASSES)
    recv_hbm, out, recv, (table, sem) = refs[:count], refs[count], refs[count + 1:2 * count + 1], refs[2 * count + 1:]
    wide = lax.axis_index("wide")
    copies = [pltpu.make_async_copy(table_hbm, table, sem.at[count])]
    copies += [pltpu.make_async_copy(recv_hbm[i], recv[i], sem.at[i]) for i in range(count)]
    for copy in copies:
        copy.start()
    out[...] = jnp.zeros_like(out)
    for copy in copies:
        copy.wait()

    def add_slot(k, carry):
        source, b = lax.div(k, 2), lax.rem(k, 2)
        r, c, there = (table[source, b, 0, lane] for lane in range(3))

        @pl.when(jnp.logical_and(there > 0, lax.div(r, 4) == wide))
        def _():
            odd = lax.rem(c, 2)
            rows = lax.rem(r, 4) * BF
            cols = lax.div(lax.rem(c, 8), 2) * 128
            for i in range(count):
                start, m = 4 * PASSES[i][0], 4 * PASSES[i][1]
                keep = iota((2 * m, 128), 1) // BF == odd
                here = recv[i][source, b, 0:2 * m].astype(F32)
                turned = pltpu.roll(here, BF, 1)
                for high in range(2):
                    part = jnp.where(keep, jnp.where(odd == high, here, turned), 0.0)
                    for low in range(2):
                        at = (2 * high + low, pl.ds(rows + start, m), pl.ds(cols, 128))
                        out[at] = out[at] + part[low * m:(low + 1) * m]
        return carry

    lax.fori_loop(0, 2 * N_WIDE, add_slot, 0)


def local(density, coefficients, task_blocks, task_live):
    any_space = pl.BlockSpec(memory_space=pl.ANY)
    smem = pl.BlockSpec(memory_space=pltpu.SMEM)
    dma = pltpu.SemaphoreType.DMA
    count = len(PASSES)
    sizes = [8 * groups for _, groups in PASSES]
    sent = [size + 16 * (i == 0) for i, size in enumerate(sizes)]
    *recv, table = pl.pallas_call(
        exchange_kernel,
        out_shape=[jax.ShapeDtypeStruct((N_WIDE, 2, size, 128), BF16) for size in sent]
        + [jax.ShapeDtypeStruct((N_WIDE, 2, 1, 128), jnp.int32)],
        in_specs=[any_space, any_space, smem, smem],
        out_specs=[any_space] * (count + 1),
        scratch_shapes=[pltpu.VMEM((SLOTS, size, 128), BF16) for size in sizes]
        + [pltpu.VMEM((N_NARROW, 2, size, 128), BF16) for size in sent]
        + [
            pltpu.VMEM((SLOTS, AUXP, BF * BF), BF16),
            pltpu.VMEM((4, 4, NDM, BF, 128), BF16),
            pltpu.VMEM((8, 128), jnp.int32),
            pltpu.VMEM((8, 128), jnp.int32),
            pltpu.SMEM((8, 128), jnp.int32),
            pltpu.VMEM((N_WIDE, 8, 128), jnp.int32),
            pltpu.SMEM((N_WIDE, 1, 128), jnp.int32),
            pltpu.VMEM((N_WIDE, BF, 256), BF16),
            pltpu.VMEM((N_WIDE, BF, 256), BF16),
            pltpu.VMEM((SLOTS, 4, 256, 256), BF16),
            pltpu.VMEM((256, 256), BF16),
            pltpu.VMEM((max(sizes) // 2, 256, AUXP), BF16),
            pltpu.VMEM((N_WIDE, 2, 16, 128), BF16),
            pltpu.VMEM((N_WIDE, 2, 8, 128), jnp.int32),
            dma((SLOTS,)), dma((16,)), dma((2,)),
            dma, dma, dma, dma, dma((count, 2)), dma((count,)),
        ],
        compiler_params=pltpu.CompilerParams(
            collective_id=0, has_side_effects=True, vmem_limit_bytes=56 * 2**20
        ),
        name="exchange",
    )(density, coefficients, task_blocks.T, task_live)
    return pl.pallas_call(
        scatter_kernel,
        out_shape=jax.ShapeDtypeStruct(density.shape, F32),
        in_specs=[any_space] * (count + 1),
        out_specs=pl.BlockSpec(memory_space=pltpu.VMEM),
        scratch_shapes=[pltpu.VMEM((N_WIDE, 2, size, 128), BF16) for size in sent]
        + [
            pltpu.SMEM((N_WIDE, 2, 1, 128), jnp.int32),
            dma((count + 1,)),
        ],
        compiler_params=pltpu.CompilerParams(vmem_limit_bytes=60 * 2**20),
        name="scatter",
    )(table, *recv)


def solution(mesh):
    in_specs = (
        P(None, "wide", "narrow"),
        P(("wide", "narrow"), None, None),
        P(("wide", "narrow"), None),
        P(("wide", "narrow")),
    )
    out_specs = P(None, "wide", "narrow")
    return jax.shard_map(local, mesh=mesh, in_specs=in_specs, out_specs=out_specs, check_vma=False)
```

```python
import jax
import jax.numpy as jnp
from jax import lax
from jax.experimental import pallas as pl
from jax.experimental.pallas import tpu as pltpu
from jax.sharding import PartitionSpec as P

BF = 64
AUXP = 256
NDM = 4
SLOTS = 8
N_WIDE = 16
N_NARROW = 8
BF16 = jnp.bfloat16
F32 = jnp.float32
MESH = pl.DeviceIdType.MESH
PASSES = ((0, 10), (10, 6))
NT = (((1,), (1,)), ((), ()))
NN = (((1,), (0,)), ((), ()))


def iota(shape, dim):
    return lax.broadcasted_iota(jnp.int32, shape, dim)


def one_hot(hit):
    return jnp.where(hit, 1.0, 0.0).astype(BF16)


def build_info(blocks, live):
    lane = iota((8, 128), 1)
    info = jnp.full((8, 128), -1, jnp.int32)
    alive = lane * 0 + live[0]
    for t in range(SLOTS):
        r, c = blocks[0, t], blocks[1, t]
        info = jnp.where((lane == lax.div(c, 4)) & (t < alive), r * 64 + c, info)
    return info


def build_plan(blocks, info, first):
    lane = iota((8, 128), 1)
    row = iota((8, 128), 0)
    stripes = [lax.div(blocks[1, t], 4) for t in range(SLOTS)]
    keys = [lax.rem(stripe + N_WIDE - first, N_WIDE) for stripe in stripes]
    plan = jnp.where(row == 0, info, 0)
    for t in range(SLOTS):
        place = sum((keys[u] < keys[t]).astype(jnp.int32) for u in range(SLOTS) if u != t)
        plan = jnp.where((row == 1) & (lane == stripes[t]), place, plan)
        plan = jnp.where((row == 2) & (lane == place), t, plan)
        plan = jnp.where((row == 3) & (lane == place), keys[t], plan)
    return plan


def pack_block(dens, code):
    code = jnp.maximum(code, 0)
    r, c = lax.div(code, 64), lax.rem(code, 64)
    pair = dens[lax.rem(c, 4), lax.div(lax.rem(r, 8), 2)].astype(F32)
    lane = iota((BF, 128), 1)
    odd = lane * 0 + lax.rem(r, 2) == 1
    low = lane < BF
    halves = []
    for d in range(0, NDM, 2):
        stays = jnp.where(odd, pair[d + 1], pair[d])
        moves = pltpu.roll(jnp.where(odd, pair[d], pair[d + 1]), BF, 1)
        halves.append(jnp.where(odd == low, moves, stays))
    return jnp.concatenate(halves, axis=1).astype(BF16)


def spread_block(block, perm, dz):
    tall = jnp.concatenate([block] * 4, axis=0)
    turned = lax.dot_general(perm[...], tall, NT, preferred_element_type=F32).astype(BF16)
    part = iota((256, 256), 1) // BF
    for q in range(4):
        dz[q] = jnp.where(part == q, turned, jnp.zeros_like(turned))


def first_step(coef, t, dz, half, start, groups):
    tall = jnp.concatenate(
        [coef[t, :, g * 256:(g + 1) * 256] for g in range(start, start + groups)], axis=0
    )
    for q in range(4):
        rows = lax.dot_general(dz[q], tall, NT, preferred_element_type=F32).astype(BF16)
        for g in range(groups):
            half[g * 4 + q] = rows[:, g * 256:(g + 1) * 256]


def second_step(coef, t, half, groups):
    m = 4 * groups
    left = jnp.concatenate(
        [half[0:m, j * 16:(j + 1) * 16, :].reshape(m * 16, AUXP) for j in range(16)], axis=1
    )
    right = jnp.concatenate([coef[t, :, j * 256:(j + 1) * 256] for j in range(16)], axis=0)
    full = lax.dot_general(left, right, NN, preferred_element_type=F32)
    full = full.reshape(m, 2, 8, 256)
    both = full[:, 0, :, :128] + full[:, 1, :, 128:]
    keep = iota((8, 128), 0) // 4 == iota((8, 128), 1) // BF
    both = jnp.where(keep[None], both, 0.0)
    folded = both + pltpu.roll(pltpu.roll(both, BF, 2), 4, 1)
    flat = folded.reshape(m * 8, 128).astype(BF16)
    i, k = iota((2 * m, m * 8), 0), iota((2 * m, m * 8), 1)
    even = one_hot(k == (i % m) * 8 + i // m)
    odd = one_hot(k == (i % m) * 8 + 6 + i // m)
    even = lax.dot_general(even, flat, NN, preferred_element_type=F32)
    odd = lax.dot_general(odd, flat, NN, preferred_element_type=F32)
    return jnp.where(iota((2 * m, 128), 1) < BF, even, odd).astype(BF16)


def label(code):
    lane = iota((16, 128), 1)
    code = lane * 0 + code
    r, c = lax.div(code, jnp.full_like(code, 64)), lax.rem(code, jnp.full_like(code, 64))
    value = jnp.where(lane == 0, r, jnp.where(lane == 1, c, jnp.where(code >= 0, 1, 0)))
    return value.astype(F32).astype(BF16)


def exchange_kernel(
    dens_hbm, coef_hbm, blocks, live, *refs
):
    count = len(PASSES)
    recvs, (table, *refs) = refs[:count], refs[count:]
    terms, slots, refs = refs[:count], refs[count:2 * count], refs[2 * count:]
    (
        coef, dens, info, plan, own, codes, codes_sm, dsend, dblk, dz, perm, half, labels, found, coef_sem, dens_sem, small_sem,
        code_send, code_recv, d_send, d_recv, t_send, t_recv,
    ) = refs
    w = lax.axis_index("wide")
    n = lax.axis_index("narrow")
    src_n = lax.div(w, 2)
    base = lax.div(w, 2)

    def dens_copy(k):
        i, j = k // 4, k % 4
        return pltpu.make_async_copy(
            dens_hbm.at[:, pl.ds(i * BF, BF), pl.ds(j * 128, 128)], dens.at[i, j], dens_sem.at[k]
        )

    for k in range(16):
        dens_copy(k).start()
    info[...] = build_info(blocks, live)

    barrier = pltpu.get_barrier_semaphore()

    for k in range(1, N_WIDE):
        pl.semaphore_signal(barrier, inc=1, device_id=(lax.rem(w + k, N_WIDE), n), device_id_type=MESH)
    for k in range(N_WIDE):

        @pl.when(jnp.logical_or(k != w, src_n != n))
        def _():
            pl.semaphore_signal(barrier, inc=1, device_id=(k, src_n), device_id_type=MESH)

    def coef_copy(t):
        return pltpu.make_async_copy(coef_hbm.at[t], coef.at[t], coef_sem.at[t])

    for t in range(SLOTS):
        coef_copy(t).start()

    @pl.when(src_n == n)
    def _():
        pl.semaphore_wait(barrier, 2 * N_WIDE - 2)

    @pl.when(src_n != n)
    def _():
        pl.semaphore_wait(barrier, 2 * N_WIDE - 1)

    def code_copy(k):
        peer = lax.rem(w + k, N_WIDE)
        return pltpu.make_async_remote_copy(
            src_ref=info, dst_ref=codes.at[w], send_sem=code_send, recv_sem=code_recv,
            device_id=(peer, n), device_id_type=MESH,
        )

    for k in range(1, N_WIDE):
        code_copy(k).start()
    codes[w] = info[...]

    plan[...] = build_plan(blocks, info[...], 2 * base)
    own_copy = pltpu.make_async_copy(plan, own, small_sem.at[0])
    own_copy.start()

    i, k = iota((256, 256), 0), iota((256, 256), 1)
    perm[...] = one_hot(k == (i % 4) * BF + i // 4)

    most = pl.ds(0, N_WIDE - 1)
    pltpu.make_async_copy(codes.at[most], codes.at[most], code_recv).wait()
    codes_copy = pltpu.make_async_copy(codes.at[:, pl.ds(0, 1), :], codes_sm, small_sem.at[1])
    codes_copy.start()
    for k in range(16):
        dens_copy(k).wait()
    own_copy.wait()
    codes_copy.wait()

    def peer_of(k):
        return 2 * lax.rem(base - k // 2 + N_NARROW, N_NARROW) + k % 2

    def block_copy(k):
        return pltpu.make_async_remote_copy(
            src_ref=dsend.at[k], dst_ref=dblk.at[w - 2 * base + k // 2 * 2], send_sem=d_send,
            recv_sem=d_recv.at[w - 2 * base + k // 2 * 2], device_id=(peer_of(k), n), device_id_type=MESH,
        )

    near = SLOTS + 2
    for k in range(0, near, 2):
        for j in (k, k + 1):
            dsend[j] = pack_block(dens, codes_sm[peer_of(j), 0, w])
        for j in (k, k + 1):
            if j > 1:
                block_copy(j).start()
                continue

            @pl.when(peer_of(j) == w)
            def _():
                dblk[w - 2 * base] = dsend[j]

            @pl.when(peer_of(j) != w)
            def _():
                block_copy(j).start()

    for k in range(near, N_WIDE):
        dsend[k] = pack_block(dens, codes_sm[peer_of(k), 0, w])

    def wait_block(j):
        pltpu.make_async_copy(dblk.at[j], dblk.at[j], d_recv.at[j]).wait()

    wait_block(1 - (w - 2 * base))
    for j in range(2, SLOTS + 1):
        wait_block(j)
    for k in range(near, N_WIDE):
        block_copy(k).start()
    for t in range(SLOTS):
        coef_copy(t).wait()

    def term_copy(i, a, q):
        return pltpu.make_async_remote_copy(
            src_ref=slots[i].at[q], dst_ref=recvs[i].at[w],
            send_sem=t_send.at[i, a], recv_sem=t_recv.at[i],
            device_id=(2 * n + a, q), device_id_type=MESH,
        )

    def is_self(a, q):
        return jnp.logical_and(q == n, 2 * n + a == w)

    def fill_slots(i, k):
        m = 4 * PASSES[i][1]
        q = lax.rem(base + k, N_NARROW)
        for b in range(2):
            slots[i][q, b, 0:2 * m] = terms[i][own[1, 2 * q + b]]
            if i == 0:
                slots[i][q, b, 2 * m:2 * m + 16] = label(own[0, 2 * q + b])

    def send_slots(i, k):
        q = lax.rem(base + k, N_NARROW)
        for a in range(2):

            @pl.when(is_self(a, q))
            def _():
                pltpu.make_async_copy(slots[i].at[q], recvs[i].at[w], t_recv.at[i]).start()

            @pl.when(jnp.logical_not(is_self(a, q)))
            def _():
                term_copy(i, a, q).start()

    def label_copy():
        m = 4 * PASSES[0][1]
        return pltpu.make_async_copy(recvs[0].at[:, :, pl.ds(2 * m, 16), :], labels, small_sem.at[0])

    def table_copy():
        return pltpu.make_async_copy(found.at[:, :, pl.ds(0, 1), :], table, small_sem.at[1])

    def run_pass(i):
        start, groups = PASSES[i]

        def task(k, carry):
            t = own[2, k]
            if i == 0:
                @pl.when(k > 0)
                def _():
                    wait_block(SLOTS + k)

                block = dblk[k]
                away = iota((BF, 256), 0) * 0 + own[3, k]
                for j in range(1, SLOTS + 1):
                    block = jnp.where(away == k + j, dblk[k + j], block)
                spread_block(block, perm, dz.at[k])
            first_step(coef, t, dz.at[k], half, start, groups)

            def finish():
                terms[i][k] = second_step(coef, t, half, groups)

            if groups > 4:
                finish()
            else:
                pl.when(k >= 0)(finish)

            @pl.when(lax.rem(k, 2) == 1)
            def _():
                fill_slots(i, lax.div(k, 2))
                send_slots(i, lax.div(k, 2))

            if i == 1:

                @pl.when(k == SLOTS - 2)
                def _():
                    pltpu.make_async_copy(recvs[0], recvs[0], t_recv.at[0]).wait()
                    label_copy().start()

                @pl.when(k == SLOTS - 1)
                def _():
                    label_copy().wait()
                    found[...] = labels[:, :, 0:8, :].astype(F32).astype(jnp.int32)
                    table_copy().start()
            return carry

        lax.fori_loop(0, SLOTS, task, 0)

        for k in range(SLOTS // 2, N_NARROW):
            fill_slots(i, k)
        for k in range(SLOTS // 2, N_NARROW):
            send_slots(i, k)

    for i in range(count):
        run_pass(i)

    def wait_sent(i):
        for a in range(2):

            @pl.when(2 * n + a == w)
            def _():
                some = slots[i].at[pl.ds(0, N_NARROW - 1)]
                pltpu.make_async_copy(some, some, t_send.at[i, a]).wait()

            @pl.when(2 * n + a != w)
            def _():
                pltpu.make_async_copy(slots[i], slots[i], t_send.at[i, a]).wait()

    pltpu.make_async_copy(codes.at[most], codes.at[most], code_send).wait()
    pltpu.make_async_copy(dblk.at[most], dblk.at[most], d_send).wait()
    wait_sent(0)
    table_copy().wait()
    pltpu.make_async_copy(recvs[1], recvs[1], t_recv.at[1]).wait()
    wait_sent(1)


def scatter_kernel(table_hbm, *refs):
    count = len(PASSES)
    recv_hbm, out, recv, (table, sem) = refs[:count], refs[count], refs[count + 1:2 * count + 1], refs[2 * count + 1:]
    wide = lax.axis_index("wide")
    copies = [pltpu.make_async_copy(table_hbm, table, sem.at[count])]
    copies += [pltpu.make_async_copy(recv_hbm[i], recv[i], sem.at[i]) for i in range(count)]
    for copy in copies:
        copy.start()
    out[...] = jnp.zeros_like(out)
    for copy in copies:
        copy.wait()

    def add_slot(k, carry):
        source, b = lax.div(k, 2), lax.rem(k, 2)
        r, c, there = (table[source, b, 0, lane] for lane in range(3))

        @pl.when(jnp.logical_and(there > 0, lax.div(r, 4) == wide))
        def _():
            odd = lax.rem(c, 2)
            rows = lax.rem(r, 4) * BF
            cols = lax.div(lax.rem(c, 8), 2) * 128
            for i in range(count):
                start, m = 4 * PASSES[i][0], 4 * PASSES[i][1]
                keep = iota((2 * m, 128), 1) // BF == odd
                here = recv[i][source, b, 0:2 * m].astype(F32)
                turned = pltpu.roll(here, BF, 1)
                for high in range(2):
                    part = jnp.where(keep, jnp.where(odd == high, here, turned), 0.0)
                    for low in range(2):
                        at = (2 * high + low, pl.ds(rows + start, m), pl.ds(cols, 128))
                        out[at] = out[at] + part[low * m:(low + 1) * m]
        return carry

    lax.fori_loop(0, 2 * N_WIDE, add_slot, 0)


def local(density, coefficients, task_blocks, task_live):
    any_space = pl.BlockSpec(memory_space=pl.ANY)
    smem = pl.BlockSpec(memory_space=pltpu.SMEM)
    dma = pltpu.SemaphoreType.DMA
    count = len(PASSES)
    sizes = [8 * groups for _, groups in PASSES]
    sent = [size + 16 * (i == 0) for i, size in enumerate(sizes)]
    *recv, table = pl.pallas_call(
        exchange_kernel,
        out_shape=[jax.ShapeDtypeStruct((N_WIDE, 2, size, 128), BF16) for size in sent]
        + [jax.ShapeDtypeStruct((N_WIDE, 2, 1, 128), jnp.int32)],
        in_specs=[any_space, any_space, smem, smem],
        out_specs=[any_space] * (count + 1),
        scratch_shapes=[pltpu.VMEM((SLOTS, size, 128), BF16) for size in sizes]
        + [pltpu.VMEM((N_NARROW, 2, size, 128), BF16) for size in sent]
        + [
            pltpu.VMEM((SLOTS, AUXP, BF * BF), BF16),
            pltpu.VMEM((4, 4, NDM, BF, 128), BF16),
            pltpu.VMEM((8, 128), jnp.int32),
            pltpu.VMEM((8, 128), jnp.int32),
            pltpu.SMEM((8, 128), jnp.int32),
            pltpu.VMEM((N_WIDE, 8, 128), jnp.int32),
            pltpu.SMEM((N_WIDE, 1, 128), jnp.int32),
            pltpu.VMEM((N_WIDE, BF, 256), BF16),
            pltpu.VMEM((N_WIDE, BF, 256), BF16),
            pltpu.VMEM((SLOTS, 4, 256, 256), BF16),
            pltpu.VMEM((256, 256), BF16),
            pltpu.VMEM((max(sizes) // 2, 256, AUXP), BF16),
            pltpu.VMEM((N_WIDE, 2, 16, 128), BF16),
            pltpu.VMEM((N_WIDE, 2, 8, 128), jnp.int32),
            dma((SLOTS,)), dma((16,)), dma((2,)),
            dma, dma, dma, dma((N_WIDE,)), dma((count, 2)), dma((count,)),
        ],
        compiler_params=pltpu.CompilerParams(
            collective_id=0, has_side_effects=True, vmem_limit_bytes=56 * 2**20
        ),
        name="exchange",
    )(density, coefficients, task_blocks.T, task_live)
    return pl.pallas_call(
        scatter_kernel,
        out_shape=jax.ShapeDtypeStruct(density.shape, F32),
        in_specs=[any_space] * (count + 1),
        out_specs=pl.BlockSpec(memory_space=pltpu.VMEM),
        scratch_shapes=[pltpu.VMEM((N_WIDE, 2, size, 128), BF16) for size in sent]
        + [
            pltpu.SMEM((N_WIDE, 2, 1, 128), jnp.int32),
            dma((count + 1,)),
        ],
        compiler_params=pltpu.CompilerParams(vmem_limit_bytes=60 * 2**20),
        name="scatter",
    )(table, *recv)


def solution(mesh):
    in_specs = (
        P(None, "wide", "narrow"),
        P(("wide", "narrow"), None, None),
        P(("wide", "narrow"), None),
        P(("wide", "narrow")),
    )
    out_specs = P(None, "wide", "narrow")
    return jax.shard_map(local, mesh=mesh, in_specs=in_specs, out_specs=out_specs, check_vma=False)
```

```python
import functools

import jax
import jax.numpy as jnp
from jax import lax
from jax.experimental import pallas as pl
from jax.experimental.pallas import tpu as pltpu
from jax.sharding import PartitionSpec as P

BF = 64
AUXP = 256
NDM = 4
SLOTS = 8
N_WIDE = 16
N_NARROW = 8
BF16 = jnp.bfloat16
F32 = jnp.float32
MESH = pl.DeviceIdType.MESH
PASSES = ((0, 10), (10, 6))
NT = (((1,), (1,)), ((), ()))
NN = (((1,), (0,)), ((), ()))


def iota(shape, dim):
    return lax.broadcasted_iota(jnp.int32, shape, dim)


def one_hot(hit):
    return jnp.where(hit, 1.0, 0.0).astype(BF16)


def build_info(blocks, live):
    lane = iota((8, 128), 1)
    info = jnp.full((8, 128), -1, jnp.int32)
    alive = lane * 0 + live[0]
    for t in range(SLOTS):
        r, c = blocks[0, t], blocks[1, t]
        info = jnp.where((lane == lax.div(c, 4)) & (t < alive), r * 64 + c, info)
    return info


def build_plan(blocks, info, first):
    lane = iota((8, 128), 1)
    row = iota((8, 128), 0)
    stripes = [lax.div(blocks[1, t], 4) for t in range(SLOTS)]
    keys = [lax.rem(stripe + N_WIDE - first, N_WIDE) for stripe in stripes]
    plan = jnp.where(row == 0, info, 0)
    for t in range(SLOTS):
        place = sum((keys[u] < keys[t]).astype(jnp.int32) for u in range(SLOTS) if u != t)
        plan = jnp.where((row == 1) & (lane == stripes[t]), place, plan)
        plan = jnp.where((row == 2) & (lane == place), t, plan)
        plan = jnp.where((row == 3) & (lane == place), keys[t], plan)
    return plan


def pack_block(dens, code):
    code = jnp.maximum(code, 0)
    r, c = lax.div(code, 64), lax.rem(code, 64)
    pair = dens[lax.rem(c, 4), lax.div(lax.rem(r, 8), 2)].astype(F32)
    lane = iota((BF, 128), 1)
    odd = lane * 0 + lax.rem(r, 2) == 1
    low = lane < BF
    halves = []
    for d in range(0, NDM, 2):
        stays = jnp.where(odd, pair[d + 1], pair[d])
        moves = pltpu.roll(jnp.where(odd, pair[d], pair[d + 1]), BF, 1)
        halves.append(jnp.where(odd == low, moves, stays))
    return jnp.concatenate(halves, axis=1).astype(BF16)


def spread_block(block, perm, dz):
    tall = jnp.concatenate([block] * 4, axis=0)
    turned = lax.dot_general(perm[...], tall, NT, preferred_element_type=F32).astype(BF16)
    part = iota((256, 256), 1) // BF
    for q in range(4):
        dz[q] = jnp.where(part == q, turned, jnp.zeros_like(turned))


def first_step(coef, t, dz, half, start, groups):
    tall = jnp.concatenate(
        [coef[t, :, g * 256:(g + 1) * 256] for g in range(start, start + groups)], axis=0
    )
    for q in range(4):
        rows = lax.dot_general(dz[q], tall, NT, preferred_element_type=F32).astype(BF16)
        for g in range(groups):
            half[g * 4 + q] = rows[:, g * 256:(g + 1) * 256]


def second_step(coef, t, half, groups):
    m = 4 * groups
    left = jnp.concatenate(
        [half[0:m, j * 16:(j + 1) * 16, :].reshape(m * 16, AUXP) for j in range(16)], axis=1
    )
    right = jnp.concatenate([coef[t, :, j * 256:(j + 1) * 256] for j in range(16)], axis=0)
    full = lax.dot_general(left, right, NN, preferred_element_type=F32)
    full = full.reshape(m, 2, 8, 256)
    both = full[:, 0, :, :128] + full[:, 1, :, 128:]
    keep = iota((8, 128), 0) // 4 == iota((8, 128), 1) // BF
    both = jnp.where(keep[None], both, 0.0)
    folded = both + pltpu.roll(pltpu.roll(both, BF, 2), 4, 1)
    flat = folded.reshape(m * 8, 128).astype(BF16)
    i, k = iota((2 * m, m * 8), 0), iota((2 * m, m * 8), 1)
    even = one_hot(k == (i % m) * 8 + i // m)
    odd = one_hot(k == (i % m) * 8 + 6 + i // m)
    even = lax.dot_general(even, flat, NN, preferred_element_type=F32)
    odd = lax.dot_general(odd, flat, NN, preferred_element_type=F32)
    return jnp.where(iota((2 * m, 128), 1) < BF, even, odd).astype(BF16)


def label(code):
    lane = iota((16, 128), 1)
    code = lane * 0 + code
    r, c = lax.div(code, jnp.full_like(code, 64)), lax.rem(code, jnp.full_like(code, 64))
    value = jnp.where(lane == 0, r, jnp.where(lane == 1, c, jnp.where(code >= 0, 1, 0)))
    return value.astype(F32).astype(BF16)


def exchange_kernel(
    dens_hbm, coef_hbm, blocks, live, *refs
):
    count = len(PASSES)
    recvs, (table, *refs) = refs[:count], refs[count:]
    terms, slots, refs = refs[:count], refs[count:2 * count], refs[2 * count:]
    (
        coef, dens, info, plan, own, codes, codes_sm, dsend, dblk, dz, perm, half, labels, found, coef_sem, dens_sem, small_sem,
        code_send, code_recv, d_send, d_recv, t_send, t_recv,
    ) = refs
    w = lax.axis_index("wide")
    n = lax.axis_index("narrow")
    src_n = lax.div(w, 2)
    base = lax.div(w, 2)

    def dens_copy(k):
        i, j = k // 4, k % 4
        return pltpu.make_async_copy(
            dens_hbm.at[:, pl.ds(i * BF, BF), pl.ds(j * 128, 128)], dens.at[i, j], dens_sem.at[k]
        )

    for k in range(16):
        dens_copy(k).start()
    info[...] = build_info(blocks, live)

    barrier = pltpu.get_barrier_semaphore()

    for k in range(1, N_WIDE):
        pl.semaphore_signal(barrier, inc=1, device_id=(lax.rem(w + k, N_WIDE), n), device_id_type=MESH)
    for k in range(N_WIDE):

        @pl.when(jnp.logical_or(k != w, src_n != n))
        def _():
            pl.semaphore_signal(barrier, inc=1, device_id=(k, src_n), device_id_type=MESH)

    def coef_copy(t):
        return pltpu.make_async_copy(coef_hbm.at[t], coef.at[t], coef_sem.at[t])

    for t in range(SLOTS):
        coef_copy(t).start()

    @pl.when(src_n == n)
    def _():
        pl.semaphore_wait(barrier, 2 * N_WIDE - 2)

    @pl.when(src_n != n)
    def _():
        pl.semaphore_wait(barrier, 2 * N_WIDE - 1)

    def code_copy(k):
        peer = lax.rem(w + k, N_WIDE)
        return pltpu.make_async_remote_copy(
            src_ref=info, dst_ref=codes.at[w], send_sem=code_send, recv_sem=code_recv,
            device_id=(peer, n), device_id_type=MESH,
        )

    for k in range(1, N_WIDE):
        code_copy(k).start()
    codes[w] = info[...]

    plan[...] = build_plan(blocks, info[...], 2 * base)
    own_copy = pltpu.make_async_copy(plan, own, small_sem.at[0])
    own_copy.start()

    i, k = iota((256, 256), 0), iota((256, 256), 1)
    perm[...] = one_hot(k == (i % 4) * BF + i // 4)

    most = pl.ds(0, N_WIDE - 1)
    pltpu.make_async_copy(codes.at[most], codes.at[most], code_recv).wait()
    codes_copy = pltpu.make_async_copy(codes.at[:, pl.ds(0, 1), :], codes_sm, small_sem.at[1])
    codes_copy.start()
    for k in range(16):
        dens_copy(k).wait()
    own_copy.wait()
    codes_copy.wait()

    def peer_of(k):
        return 2 * lax.rem(base - k // 2 + N_NARROW, N_NARROW) + k % 2

    def block_copy(k):
        return pltpu.make_async_remote_copy(
            src_ref=dsend.at[k], dst_ref=dblk.at[w - 2 * base + k // 2 * 2], send_sem=d_send,
            recv_sem=d_recv.at[w - 2 * base + k // 2 * 2], device_id=(peer_of(k), n), device_id_type=MESH,
        )

    near = SLOTS + 2
    for k in range(0, near, 2):
        for j in (k, k + 1):
            dsend[j] = pack_block(dens, codes_sm[peer_of(j), 0, w])
        for j in (k, k + 1):
            if j > 1:
                block_copy(j).start()
                continue

            @pl.when(peer_of(j) == w)
            def _():
                dblk[w - 2 * base] = dsend[j]

            @pl.when(peer_of(j) != w)
            def _():
                block_copy(j).start()

    for k in range(near, N_WIDE):
        dsend[k] = pack_block(dens, codes_sm[peer_of(k), 0, w])

    def wait_block(j):
        pltpu.make_async_copy(dblk.at[j], dblk.at[j], d_recv.at[j]).wait()

    wait_block(1 - (w - 2 * base))
    for j in range(2, SLOTS + 1):
        wait_block(j)
    for k in range(near, N_WIDE):
        block_copy(k).start()
    for t in range(SLOTS):
        coef_copy(t).wait()

    def term_copy(i, a, q):
        return pltpu.make_async_remote_copy(
            src_ref=slots[i].at[q], dst_ref=recvs[i].at[w],
            send_sem=t_send.at[i, a], recv_sem=t_recv.at[i],
            device_id=(2 * n + a, q), device_id_type=MESH,
        )

    def is_self(a, q):
        return jnp.logical_and(q == n, 2 * n + a == w)

    def fill_slots(i, k):
        m = 4 * PASSES[i][1]
        q = lax.rem(base + k, N_NARROW)
        for b in range(2):
            slots[i][q, b, 0:2 * m] = terms[i][own[1, 2 * q + b]]
            if i == 0:
                slots[i][q, b, 2 * m:2 * m + 16] = label(own[0, 2 * q + b])

    def send_slots(i, k):
        q = lax.rem(base + k, N_NARROW)
        for a in range(2):

            @pl.when(is_self(a, q))
            def _():
                pltpu.make_async_copy(slots[i].at[q], recvs[i].at[w], t_recv.at[i]).start()

            @pl.when(jnp.logical_not(is_self(a, q)))
            def _():
                term_copy(i, a, q).start()

    def label_copy():
        m = 4 * PASSES[0][1]
        return pltpu.make_async_copy(recvs[0].at[:, :, pl.ds(2 * m, 16), :], labels, small_sem.at[0])

    def table_copy():
        return pltpu.make_async_copy(found.at[:, :, pl.ds(0, 1), :], table, small_sem.at[1])

    def run_pass(i):
        start, groups = PASSES[i]

        def task(k, carry):
            t = own[2, k]
            if i == 0:
                @pl.when(k > 0)
                def _():
                    wait_block(SLOTS + k)

                block = dblk[k]
                away = iota((BF, 256), 0) * 0 + own[3, k]
                for j in range(1, SLOTS + 1):
                    block = jnp.where(away == k + j, dblk[k + j], block)
                spread_block(block, perm, dz.at[k])
            first_step(coef, t, dz.at[k], half, start, groups)

            def finish():
                terms[i][k] = second_step(coef, t, half, groups)

            if groups > 4:
                finish()
            else:
                pl.when(k >= 0)(finish)

            @pl.when(lax.rem(k, 2) == 1)
            def _():
                fill_slots(i, lax.div(k, 2))
                send_slots(i, lax.div(k, 2))

            if i == 1:

                @pl.when(k == SLOTS - 2)
                def _():
                    pltpu.make_async_copy(recvs[0], recvs[0], t_recv.at[0]).wait()
                    label_copy().start()

                @pl.when(k == SLOTS - 1)
                def _():
                    label_copy().wait()
                    found[...] = labels[:, :, 0:8, :].astype(F32).astype(jnp.int32)
                    table_copy().start()
            return carry

        lax.fori_loop(0, SLOTS, task, 0)

        for k in range(SLOTS // 2, N_NARROW):
            fill_slots(i, k)
        for k in range(SLOTS // 2, N_NARROW):
            send_slots(i, k)

    for i in range(count):
        run_pass(i)

    def wait_sent(i):
        for a in range(2):

            @pl.when(2 * n + a == w)
            def _():
                some = slots[i].at[pl.ds(0, N_NARROW - 1)]
                pltpu.make_async_copy(some, some, t_send.at[i, a]).wait()

            @pl.when(2 * n + a != w)
            def _():
                pltpu.make_async_copy(slots[i], slots[i], t_send.at[i, a]).wait()

    pltpu.make_async_copy(codes.at[most], codes.at[most], code_send).wait()
    pltpu.make_async_copy(dblk.at[most], dblk.at[most], d_send).wait()
    wait_sent(0)
    table_copy().wait()
    pltpu.make_async_copy(recvs[1], recvs[1], t_recv.at[1]).wait()
    wait_sent(1)


def scatter_kernel(table_hbm, *refs):
    count = len(PASSES)
    recv_hbm, out_hbm, recv = refs[:count], refs[count], refs[count + 1:2 * count + 1]
    out, table, sem = refs[2 * count + 1:]
    wide = lax.axis_index("wide")
    copies = [pltpu.make_async_copy(table_hbm, table, sem.at[count])]
    copies += [pltpu.make_async_copy(recv_hbm[i], recv[i], sem.at[i]) for i in range(count)]
    for copy in copies:
        copy.start()
    out[...] = jnp.zeros_like(out)
    for copy in copies:
        copy.wait()

    def add_slot(k, carry, high):
        source, b = lax.div(k, 2), lax.rem(k, 2)
        r, c, there = (table[source, b, 0, lane] for lane in range(3))

        @pl.when(jnp.logical_and(there > 0, lax.div(r, 4) == wide))
        def _():
            odd = lax.rem(c, 2)
            rows = lax.rem(r, 4) * BF
            cols = lax.div(lax.rem(c, 8), 2) * 128
            for i in range(count):
                start, m = 4 * PASSES[i][0], 4 * PASSES[i][1]
                keep = iota((2 * m, 128), 1) // BF == odd
                here = recv[i][source, b, 0:2 * m].astype(F32)
                turned = pltpu.roll(here, BF, 1)
                part = jnp.where(keep, jnp.where(odd == high, here, turned), 0.0)
                for low in range(2):
                    at = (2 * high + low, pl.ds(rows + start, m), pl.ds(cols, 128))
                    out[at] = out[at] + part[low * m:(low + 1) * m]
        return carry

    done = []
    for high in range(2):
        lax.fori_loop(0, 2 * N_WIDE, functools.partial(add_slot, high=high), 0)
        pair = pl.ds(2 * high, 2)
        done.append(pltpu.make_async_copy(out.at[pair], out_hbm.at[pair], sem.at[count + 1 + high]))
        done[-1].start()
    for copy in done:
        copy.wait()


def local(density, coefficients, task_blocks, task_live):
    any_space = pl.BlockSpec(memory_space=pl.ANY)
    smem = pl.BlockSpec(memory_space=pltpu.SMEM)
    dma = pltpu.SemaphoreType.DMA
    count = len(PASSES)
    sizes = [8 * groups for _, groups in PASSES]
    sent = [size + 16 * (i == 0) for i, size in enumerate(sizes)]
    *recv, table = pl.pallas_call(
        exchange_kernel,
        out_shape=[jax.ShapeDtypeStruct((N_WIDE, 2, size, 128), BF16) for size in sent]
        + [jax.ShapeDtypeStruct((N_WIDE, 2, 1, 128), jnp.int32)],
        in_specs=[any_space, any_space, smem, smem],
        out_specs=[any_space] * (count + 1),
        scratch_shapes=[pltpu.VMEM((SLOTS, size, 128), BF16) for size in sizes]
        + [pltpu.VMEM((N_NARROW, 2, size, 128), BF16) for size in sent]
        + [
            pltpu.VMEM((SLOTS, AUXP, BF * BF), BF16),
            pltpu.VMEM((4, 4, NDM, BF, 128), BF16),
            pltpu.VMEM((8, 128), jnp.int32),
            pltpu.VMEM((8, 128), jnp.int32),
            pltpu.SMEM((8, 128), jnp.int32),
            pltpu.VMEM((N_WIDE, 8, 128), jnp.int32),
            pltpu.SMEM((N_WIDE, 1, 128), jnp.int32),
            pltpu.VMEM((N_WIDE, BF, 256), BF16),
            pltpu.VMEM((N_WIDE, BF, 256), BF16),
            pltpu.VMEM((SLOTS, 4, 256, 256), BF16),
            pltpu.VMEM((256, 256), BF16),
            pltpu.VMEM((max(sizes) // 2, 256, AUXP), BF16),
            pltpu.VMEM((N_WIDE, 2, 16, 128), BF16),
            pltpu.VMEM((N_WIDE, 2, 8, 128), jnp.int32),
            dma((SLOTS,)), dma((16,)), dma((2,)),
            dma, dma, dma, dma((N_WIDE,)), dma((count, 2)), dma((count,)),
        ],
        compiler_params=pltpu.CompilerParams(
            collective_id=0, has_side_effects=True, vmem_limit_bytes=56 * 2**20
        ),
        name="exchange",
    )(density, coefficients, task_blocks.T, task_live)
    return pl.pallas_call(
        scatter_kernel,
        out_shape=jax.ShapeDtypeStruct(density.shape, F32),
        in_specs=[any_space] * (count + 1),
        out_specs=any_space,
        scratch_shapes=[pltpu.VMEM((N_WIDE, 2, size, 128), BF16) for size in sent]
        + [
            pltpu.VMEM(density.shape, F32),
            pltpu.SMEM((N_WIDE, 2, 1, 128), jnp.int32),
            dma((count + 3,)),
        ],
        compiler_params=pltpu.CompilerParams(vmem_limit_bytes=60 * 2**20),
        name="scatter",
    )(table, *recv)


def solution(mesh):
    in_specs = (
        P(None, "wide", "narrow"),
        P(("wide", "narrow"), None, None),
        P(("wide", "narrow"), None),
        P(("wide", "narrow")),
    )
    out_specs = P(None, "wide", "narrow")
    return jax.shard_map(local, mesh=mesh, in_specs=in_specs, out_specs=out_specs, check_vma=False)
```
